32 devices in a mesh: mpo: 4 (over z), sec: 8 (over y, x, core).
Axes of the slice: x: 2, y: 2, z: 4, core: 2. Of those that a mesh axis runs over, the one named last changes fastest.
Arguments:
- wavefunction: bfloat16 [2, 64, 512, 512], P(None, 'sec'), may hold values from -6 to 6
- left_env: bfloat16 [8, 64, 512, 512], P('mpo', 'sec'), may hold values from -0.25 to 0.25
- right_env: bfloat16 [8, 64, 512, 512], P('mpo', 'sec'), may hold values from -0.09375 to 0.09375
- block_dims: int32 [64], P('sec'), may hold values from 128 to 512, as said below
- mpo_shift: int32 [8], P('mpo'), may hold values from -1 to 1
Outputs:
- sigma_blocks: bfloat16 [2, 64, 512, 512], P(None, 'sec', 'mpo')
The draws below stay inside these ranges and needn't reach their ends.
Inputs may be any that keep to these rules, and one draw needn't show every extreme that they name: `block_dims`: some block is full.
All inputs are finite; a program needn't handle non-finite values.
Results may differ from the reference program's by a relative error of at most 0.0049.
Values may be sent and summed in bfloat16 or wider, within the bound.
No kernel may reach another device: no remote copies, remote signals or barrier semaphores. Data moves between devices by JAX's collectives and lax.ppermute only.
A program may use at most 192 MiB of HBM per device.

```python
import jax
import jax.numpy as jnp
from jax import lax

DB = 512
KV = 2
NSEC_DEV = 8
W = 8
NSEC = 64
N_SEC = 8


def draw_block_dims(key, part):
    first_key, second_key = jax.random.split(key)
    drawn = jax.random.randint(first_key, (NSEC,), DB // 4, DB + 1)
    full_slot = jax.random.randint(second_key, (), 0, NSEC)
    slots = jnp.arange(NSEC)
    return jnp.where(slots == full_slot, DB, drawn).astype(jnp.int32)


def place_ends(values, stream_key, smallest, high):
    dims = values.shape
    place = [jax.random.randint(jax.random.fold_in(stream_key, axis), (), 0, dims[axis]) for axis in range(len(dims))]
    values = values.at[tuple(place)].set(smallest)
    longest = dims.index(max(dims))
    place[longest] = (place[longest] + 1) % dims[longest]
    return values.at[tuple(place)].set(high)


def levels(stream_key, shape, pieces, least, top_value):
    loudness, own = 1.0, jax.random.fold_in(stream_key, 6)
    for axis_at, parts in pieces:
        steps = jnp.exp(jax.random.uniform(jax.random.fold_in(own, axis_at), (parts,), jnp.float32, least / len(pieces), top_value / len(pieces)))
        loudness = loudness * jnp.repeat(steps, shape[axis_at] // parts).reshape([-1 if axis == axis_at else 1 for axis in range(len(shape))])
    return loudness


def bell_draw(own_key, dims, deviation, most, cuts=(), kind=jnp.bfloat16):
    loudness = levels(own_key, dims, cuts, -0.22, 0.18) if cuts else 1.0
    result = jax.random.normal(own_key, dims, jnp.float32) * deviation * loudness
    return jnp.minimum(jnp.maximum(result, -most), most).astype(kind)


def setup_inputs(seed: int = 0) -> dict:
    keys = jax.random.split(jax.random.key(seed), 6)
    return {
        "wavefunction": bell_draw(keys[0], (KV, NSEC, DB, DB), 1.0, 6.0, ((1, 8),)),
        "left_env": bell_draw(keys[1], (W, NSEC, DB, DB), DB ** -0.5, 0.25, ((0, 4), (1, 8))),
        "right_env": bell_draw(keys[2], (W, NSEC, DB, DB), (DB * W) ** -0.5, 0.09375, ((0, 4), (1, 8))),
        "block_dims": draw_block_dims(jax.random.fold_in(keys[5], 71), 0),
        "mpo_shift": place_ends(jax.random.randint(keys[4], (W,), -1, 2), jax.random.fold_in(keys[4], 1), -1, 1).astype(jnp.int32),
    }


def charge_order(blocks):
    trailing = blocks.shape[1:]
    return blocks.reshape((N_SEC, NSEC_DEV) + trailing).swapaxes(0, 1).reshape((NSEC,) + trailing)


def slot_order(blocks):
    trailing = blocks.shape[1:]
    return blocks.reshape((NSEC_DEV, N_SEC) + trailing).swapaxes(0, 1).reshape((NSEC,) + trailing)


def reference(wavefunction, left_env, right_env, block_dims, mpo_shift):
    own_blocks = jnp.moveaxis(wavefunction, 1, 0)
    by_charge = charge_order(own_blocks)
    empty_block = jnp.zeros_like(by_charge[:1])
    from_lower = slot_order(jnp.concatenate([empty_block, by_charge[:-1]], axis=0))
    from_upper = slot_order(jnp.concatenate([by_charge[1:], empty_block], axis=0))
    variants = jnp.stack([from_upper, own_blocks, from_lower])

    def add_row(accumulated, inputs):
        left_row, right_row, change = inputs
        chosen = lax.dynamic_index_in_dim(variants, (change + 1).astype(jnp.int32), 0, keepdims=False)
        left_part = jnp.einsum('sab,skbc->skac', left_row.astype(jnp.float32), chosen.astype(jnp.float32)).astype(jnp.bfloat16)
        contribution = jnp.einsum('skac,scd->skad', left_part.astype(jnp.float32), right_row.astype(jnp.float32))
        return accumulated + contribution, None

    initial = jnp.zeros(own_blocks.shape, jnp.float32)
    accumulated = lax.scan(add_row, initial, (left_env, right_env, mpo_shift))[0]
    positions = jnp.arange(DB, dtype=jnp.int32)
    block_limit = block_dims[:, None, None, None]
    inside = (positions[None, None, :, None] < block_limit) & (positions[None, None, None, :] < block_limit)
    sigma_blocks = jnp.where(inside, accumulated, jnp.zeros_like(accumulated)).astype(jnp.bfloat16)
    return jnp.moveaxis(sigma_blocks, 0, 1)
```

```python
import functools

import jax
import jax.numpy as jnp
from jax import lax
from jax.experimental import pallas as pl
from jax.experimental.pallas import tpu as pltpu
from jax.sharding import PartitionSpec as P

GROUPS = 4


def apply_kernel(flags, dims, own, lower, upper, left, right, out, *, first_slot, group):
    step = pl.program_id(0)
    slot = first_slot + step
    vectors, size = own.shape[0], own.shape[2]
    chunks, rows = out.shape[0], out.shape[3]
    limit = dims[slot]
    sources = []
    for row in range(left.shape[0]):
        shift = flags[row]
        live = jnp.logical_not(
            jnp.logical_or(
                jnp.logical_and(jnp.logical_and(shift > 0, flags[left.shape[0]] == 1), slot == 0),
                jnp.logical_and(
                    jnp.logical_and(shift < 0, flags[left.shape[0] + 1] == 1), slot == group - 1
                ),
            )
        )
        sources.append((shift, live))
    for k in range(vectors):
        total = jnp.zeros((size, size), jnp.float32)
        for row, (shift, live) in enumerate(sources):
            chosen = jnp.where(
                shift > 0, lower[k, 0], jnp.where(shift < 0, upper[k, 0], own[k, 0])
            )
            chosen = jnp.where(live, chosen, jnp.zeros_like(chosen))
            part = jnp.dot(left[row, 0], chosen, preferred_element_type=jnp.float32)
            total += jnp.dot(
                part.astype(jnp.bfloat16), right[row, 0], preferred_element_type=jnp.float32
            )
        row_index = lax.broadcasted_iota(jnp.int32, (size, size), 0)
        col_index = lax.broadcasted_iota(jnp.int32, (size, size), 1)
        inside = jnp.logical_and(row_index < limit, col_index < limit)
        kept = jnp.where(inside, total, jnp.zeros_like(total)).astype(out.dtype)
        for chunk in range(chunks):
            out[chunk, k, 0] = kept[chunk * rows : (chunk + 1) * rows]


def apply_rows(flags, dims, own, lower, upper, left, right, first_slot, chunks):
    vectors, group, size, _ = lower.shape
    rows, slots = left.shape[0], left.shape[1]
    own_spec = pl.BlockSpec((vectors, 1, size, size), lambda i, *_: (0, first_slot + i, 0, 0))
    moved_spec = pl.BlockSpec((vectors, 1, size, size), lambda i, *_: (0, i, 0, 0))
    env_spec = pl.BlockSpec((rows, 1, size, size), lambda i, *_: (0, first_slot + i, 0, 0))
    return pl.pallas_call(
        functools.partial(apply_kernel, first_slot=first_slot, group=slots),
        grid_spec=pltpu.PrefetchScalarGridSpec(
            num_scalar_prefetch=2,
            grid=(group,),
            in_specs=[own_spec, moved_spec, moved_spec, env_spec, env_spec],
            out_specs=pl.BlockSpec(
                (chunks, vectors, 1, size // chunks, size), lambda i, *_: (0, 0, i, 0, 0)
            ),
        ),
        out_shape=jax.ShapeDtypeStruct(
            (chunks, vectors, group, size // chunks, size), jnp.bfloat16
        ),
        compiler_params=pltpu.CompilerParams(vmem_limit_bytes=40 * 1024 * 1024),
        cost_estimate=pl.CostEstimate(
            flops=group * vectors * rows * 4 * size**3,
            bytes_accessed=group * size * size * 2 * (4 * vectors + 2 * rows),
            transcendentals=0,
        ),
    )(flags, dims, own, lower, upper, left, right)


def body(wavefunction, left_env, right_env, block_dims, mpo_shift):
    sec_count = lax.axis_size("sec")
    sec_index = lax.axis_index("sec")
    chunks = lax.axis_size("mpo")
    slots = wavefunction.shape[1]
    is_first = (sec_index == 0).astype(jnp.int32)
    is_last = (sec_index == sec_count - 1).astype(jnp.int32)
    flags = jnp.concatenate([mpo_shift, is_first[None], is_last[None]])
    upward = [(i, (i + 1) % sec_count) for i in range(sec_count)]
    downward = [(i, (i - 1) % sec_count) for i in range(sec_count)]

    def picked(first, count, offset):
        parts = []
        for slot in range(first, first + count):
            at = jnp.clip(slot + offset, 0, slots - 1)
            parts.append(lax.dynamic_slice_in_dim(wavefunction, at, 1, 1))
        return jnp.concatenate(parts, axis=1)

    count = max(slots // GROUPS, 1)
    pieces, arrived = [], []
    for first in range(0, slots, count):
        to_upper = picked(first, count, -is_last)
        to_lower = picked(first, count, is_first)
        if len(arrived) >= 2:
            to_upper, to_lower, _ = lax.optimization_barrier((to_upper, to_lower, arrived[-2]))
        from_lower = lax.ppermute(to_upper, "sec", upward)
        from_upper = lax.ppermute(to_lower, "sec", downward)
        arrived.append((from_lower, from_upper))
        partial = apply_rows(
            flags,
            block_dims,
            wavefunction,
            from_lower,
            from_upper,
            left_env,
            right_env,
            first,
            chunks,
        )
        pieces.append(lax.psum_scatter(partial, "mpo", scatter_dimension=0))
    return jnp.concatenate(pieces, axis=1)


def solution(mesh):
    placed = (
        P(None, "sec", None, None),
        P("mpo", "sec", None, None),
        P("mpo", "sec", None, None),
        P("sec"),
        P("mpo"),
    )
    return jax.shard_map(
        body, mesh=mesh, in_specs=placed, out_specs=P(None, "sec", "mpo", None), check_vma=False
    )
```

```python
import functools

import jax
import jax.numpy as jnp
from jax import lax
from jax.experimental import pallas as pl
from jax.experimental.pallas import tpu as pltpu
from jax.sharding import PartitionSpec as P

COST = 20
PLAN = 'A1s0 D2r1 D2r0 D2r0 D1s0'


def apply_kernel(flags, dims, *refs, first_slot, slots):
    sources, (left, right, out) = refs[:-3], refs[-3:]
    step = pl.program_id(0)
    slot = first_slot + step
    rows = left.shape[0]
    vectors, size = sources[0].shape[0], sources[0].shape[2]
    chunks, slab = out.shape[0], out.shape[3]
    limit = dims[slot]
    row_index = lax.broadcasted_iota(jnp.int32, (size, size), 0)
    col_index = lax.broadcasted_iota(jnp.int32, (size, size), 1)
    inside = jnp.logical_and(row_index < limit, col_index < limit)
    for k in range(vectors):
        total = jnp.zeros((size, size), jnp.float32)
        for row in range(rows):
            pick, edge = flags[row], flags[rows + row]
            live = jnp.logical_not(
                jnp.logical_or(
                    jnp.logical_and(edge > 0, slot == 0),
                    jnp.logical_and(edge < 0, slot == slots - 1),
                )
            )
            chosen = sources[0][k, 0]
            for i in range(1, len(sources)):
                chosen = jnp.where(pick == i, sources[i][k, 0], chosen)
            chosen = jnp.where(live, chosen, jnp.zeros_like(chosen))
            part = jnp.dot(left[row, 0], chosen, preferred_element_type=jnp.float32)
            total += jnp.dot(
                part.astype(jnp.bfloat16), right[row, 0], preferred_element_type=jnp.float32
            )
        kept = jnp.where(inside, total, jnp.zeros_like(total)).astype(out.dtype)
        for chunk in range(chunks):
            out[chunk, k, 0] = kept[chunk * slab : (chunk + 1) * slab]


def apply_rows(flags, dims, own, moved, left, right, first_slot, chunks):
    vectors, group, size, _ = moved[0].shape
    rows, slots = left.shape[0], left.shape[1]
    own_spec = pl.BlockSpec((vectors, 1, size, size), lambda i, *_: (0, first_slot + i, 0, 0))
    moved_spec = pl.BlockSpec((vectors, 1, size, size), lambda i, *_: (0, i, 0, 0))
    env_spec = pl.BlockSpec((rows, 1, size, size), lambda i, *_: (0, first_slot + i, 0, 0))
    return pl.pallas_call(
        functools.partial(apply_kernel, first_slot=first_slot, slots=slots),
        grid_spec=pltpu.PrefetchScalarGridSpec(
            num_scalar_prefetch=2,
            grid=(group,),
            in_specs=[own_spec] + [moved_spec] * len(moved) + [env_spec, env_spec],
            out_specs=pl.BlockSpec(
                (chunks, vectors, 1, size // chunks, size), lambda i, *_: (0, 0, i, 0, 0)
            ),
        ),
        out_shape=jax.ShapeDtypeStruct(
            (chunks, vectors, group, size // chunks, size), jnp.bfloat16
        ),
        compiler_params=pltpu.CompilerParams(vmem_limit_bytes=40 * 1024 * 1024),
        cost_estimate=pl.CostEstimate(
            flops=COST * group * vectors * rows * 4 * size**3,
            bytes_accessed=COST * group * size * size * 2 * (4 * vectors + 2 * rows),
            transcendentals=0,
        ),
    )(flags, dims, own, *moved, left, right)


def body(wavefunction, left_env, right_env, block_dims, mpo_shift):
    sec_count, planes = lax.axis_size("sec"), lax.axis_size("mpo")
    sec_index, plane = lax.axis_index("sec"), lax.axis_index("mpo")
    slots = wavefunction.shape[1]
    is_first = (sec_index == 0).astype(jnp.int32)
    is_last = (sec_index == sec_count - 1).astype(jnp.int32)
    odd = plane % 2
    forwards = sec_index % 2 == odd

    edge = jnp.where(mpo_shift > 0, is_first, jnp.where(mpo_shift < 0, -is_last, 0))
    direct_pick = jnp.where(mpo_shift > 0, 1, jnp.where(mpo_shift < 0, 2, 0))
    shared_pick = jnp.where(
        mpo_shift == 0, 0, jnp.where((mpo_shift > 0) == (odd == 0), 1, 2)
    )
    direct_flags = jnp.concatenate([direct_pick, edge]).astype(jnp.int32)
    shared_flags = jnp.concatenate([shared_pick, edge]).astype(jnp.int32)

    upward = [(i, (i + 1) % sec_count) for i in range(sec_count)]
    downward = [(i, (i - 1) % sec_count) for i in range(sec_count)]
    both = [
        (m * sec_count + i, m * sec_count + j)
        for m in range(planes)
        for i, j in (upward if m % 2 == 0 else downward)
    ]
    passed = [
        (m * sec_count + i, (m ^ 1) * sec_count + i if i % 2 == m % 2 else m * sec_count + (i ^ 1))
        for m in range(planes)
        for i in range(sec_count)
    ]
    can_share = planes % 2 == 0 and sec_count % 2 == 0

    def picked(source, first, count, offset):
        parts = []
        for slot in range(first, first + count):
            at = jnp.clip(slot + offset, 0, slots - 1)
            parts.append(lax.dynamic_slice_in_dim(source, at, 1, 1))
        return jnp.concatenate(parts, axis=1)

    def sent_sum(partial):
        total = lax.dynamic_index_in_dim(partial, plane, 0, keepdims=False).astype(jnp.float32)
        for distance in range(1, planes):
            target = (plane + distance) % planes
            came = lax.ppermute(
                lax.dynamic_index_in_dim(partial, target, 0, keepdims=False),
                "mpo",
                [(m, (m + distance) % planes) for m in range(planes)],
            )
            total += came.astype(jnp.float32)
        return total.astype(jnp.bfloat16)

    pieces, partials, arrived = [], [], []
    first, count = 0, 0
    for fetch, width, reduce, lag in PLAN.split():
        first, count = first + count, int(width)
        source = wavefunction
        if int(lag) and len(arrived) >= int(lag):
            source, _ = lax.optimization_barrier((source, arrived[-int(lag)]))
        elif len(partials) >= 2:
            source, _ = lax.optimization_barrier((source, partials[-2]))
        if fetch == "A" and can_share:
            to_upper = picked(source, first, count, -is_last)
            to_lower = picked(source, first, count, is_first)
            fetched = lax.ppermute(
                jnp.where(odd == 0, to_upper, to_lower), ("mpo", "sec"), both
            )
            arrived.append(fetched)
            own_side = jnp.where(odd == 0, to_lower, to_upper)
            moved = (
                fetched,
                lax.ppermute(jnp.where(forwards, fetched, own_side), ("mpo", "sec"), passed),
            )
            flags = shared_flags
        else:
            from_lower = lax.ppermute(picked(source, first, count, -is_last), "sec", upward)
            from_upper = lax.ppermute(picked(source, first, count, is_first), "sec", downward)
            moved = (from_lower, from_upper)
            arrived.append(moved)
            flags = direct_flags
        partial = apply_rows(
            flags, block_dims, wavefunction, moved, left_env, right_env, first, planes
        )
        partials.append(partial)
        if reduce == "r":
            pieces.append(lax.psum_scatter(partial, "mpo", scatter_dimension=0))
        else:
            pieces.append(sent_sum(partial))
    return jnp.concatenate(pieces, axis=1)


def solution(mesh):
    placed = (
        P(None, "sec", None, None),
        P("mpo", "sec", None, None),
        P("mpo", "sec", None, None),
        P("sec"),
        P("mpo"),
    )
    return jax.shard_map(
        body, mesh=mesh, in_specs=placed, out_specs=P(None, "sec", "mpo", None), check_vma=False
    )
```

```python
import functools

import jax
import jax.numpy as jnp
from jax import lax
from jax.experimental import pallas as pl
from jax.experimental.pallas import tpu as pltpu
from jax.sharding import PartitionSpec as P

COST = 20
PLAN = 'A1s0 D2r1 D2r0 D2r0 D1s0'


def apply_kernel(flags, dims, *refs, first_slot, slots):
    sources, (left, right, out) = refs[:-3], refs[-3:]
    step = pl.program_id(0)
    slot = first_slot + step
    rows = left.shape[0]
    vectors, size = sources[0].shape[0], sources[0].shape[2]
    chunks, slab = out.shape[0], out.shape[3]
    limit = dims[slot]
    row_index = lax.broadcasted_iota(jnp.int32, (size, size), 0)
    col_index = lax.broadcasted_iota(jnp.int32, (size, size), 1)
    inside = jnp.logical_and(row_index < limit, col_index < limit)
    for k in range(vectors):
        total = jnp.zeros((size, size), jnp.float32)
        for row in range(rows):
            pick, edge = flags[row], flags[rows + row]
            live = jnp.logical_not(
                jnp.logical_or(
                    jnp.logical_and(edge > 0, slot == 0),
                    jnp.logical_and(edge < 0, slot == slots - 1),
                )
            )
            chosen = sources[0][k, 0]
            for i in range(1, len(sources)):
                chosen = jnp.where(pick == i, sources[i][k, 0], chosen)
            chosen = jnp.where(live, chosen, jnp.zeros_like(chosen))
            part = jnp.dot(left[row, 0], chosen, preferred_element_type=jnp.float32)
            total += jnp.dot(
                part.astype(jnp.bfloat16), right[row, 0], preferred_element_type=jnp.float32
            )
        kept = jnp.where(inside, total, jnp.zeros_like(total)).astype(out.dtype)
        for chunk in range(chunks):
            out[chunk, k, 0] = kept[chunk * slab : (chunk + 1) * slab]


def apply_rows(flags, dims, own, moved, left, right, first_slot, chunks):
    vectors, group, size, _ = moved[0].shape
    rows, slots = left.shape[0], left.shape[1]
    own_spec = pl.BlockSpec((vectors, 1, size, size), lambda i, *_: (0, first_slot + i, 0, 0))
    moved_spec = pl.BlockSpec((vectors, 1, size, size), lambda i, *_: (0, i, 0, 0))
    env_spec = pl.BlockSpec((rows, 1, size, size), lambda i, *_: (0, first_slot + i, 0, 0))
    return pl.pallas_call(
        functools.partial(apply_kernel, first_slot=first_slot, slots=slots),
        grid_spec=pltpu.PrefetchScalarGridSpec(
            num_scalar_prefetch=2,
            grid=(group,),
            in_specs=[own_spec] + [moved_spec] * len(moved) + [env_spec, env_spec],
            out_specs=pl.BlockSpec(
                (chunks, vectors, 1, size // chunks, size), lambda i, *_: (0, 0, i, 0, 0)
            ),
        ),
        out_shape=jax.ShapeDtypeStruct(
            (chunks, vectors, group, size // chunks, size), jnp.bfloat16
        ),
        compiler_params=pltpu.CompilerParams(vmem_limit_bytes=40 * 1024 * 1024),
        cost_estimate=pl.CostEstimate(
            flops=COST * group * vectors * rows * 4 * size**3,
            bytes_accessed=COST * group * size * size * 2 * (4 * vectors + 2 * rows),
            transcendentals=0,
        ),
    )(flags, dims, own, *moved, left, right)


def body(wavefunction, left_env, right_env, block_dims, mpo_shift):
    sec_count, planes = lax.axis_size("sec"), lax.axis_size("mpo")
    sec_index, plane = lax.axis_index("sec"), lax.axis_index("mpo")
    slots = wavefunction.shape[1]
    is_first = (sec_index == 0).astype(jnp.int32)
    is_last = (sec_index == sec_count - 1).astype(jnp.int32)
    odd = plane % 2
    forwards = sec_index % 2 == odd

    edge = jnp.where(mpo_shift > 0, is_first, jnp.where(mpo_shift < 0, -is_last, 0))
    direct_pick = jnp.where(mpo_shift > 0, 1, jnp.where(mpo_shift < 0, 2, 0))
    shared_pick = jnp.where(
        mpo_shift == 0, 0, jnp.where((mpo_shift > 0) == (odd == 0), 1, 2)
    )
    direct_flags = jnp.concatenate([direct_pick, edge]).astype(jnp.int32)
    shared_flags = jnp.concatenate([shared_pick, edge]).astype(jnp.int32)

    upward = [(i, (i + 1) % sec_count) for i in range(sec_count)]
    downward = [(i, (i - 1) % sec_count) for i in range(sec_count)]
    both = [
        (m * sec_count + i, m * sec_count + j)
        for m in range(planes)
        for i, j in (upward if m % 2 == 0 else downward)
    ]
    passed = [
        (m * sec_count + i, (m ^ 1) * sec_count + i if i % 2 == m % 2 else m * sec_count + (i ^ 1))
        for m in range(planes)
        for i in range(sec_count)
    ]
    can_share = planes % 2 == 0 and sec_count % 2 == 0

    def picked(source, first, count, offset):
        step = -1 if offset is is_last else 1
        parts = [
            lax.slice_in_dim(source, at, at + 1, axis=1)
            for at in (min(max(slot + step, 0), slots - 1) for slot in range(first, first + count))
        ]
        plain = lax.slice_in_dim(source, first, first + count, axis=1)
        if 0 <= first + step and first + step + count <= slots:
            moved = lax.slice_in_dim(source, first + step, first + step + count, axis=1)
        else:
            moved = jnp.concatenate(parts, axis=1)
        return jnp.where(offset > 0, moved, plain)

    def sent_sum(partial):
        total = lax.dynamic_index_in_dim(partial, plane, 0, keepdims=False).astype(jnp.float32)
        for distance in range(1, planes):
            target = (plane + distance) % planes
            came = lax.ppermute(
                lax.dynamic_index_in_dim(partial, target, 0, keepdims=False),
                "mpo",
                [(m, (m + distance) % planes) for m in range(planes)],
            )
            total += came.astype(jnp.float32)
        return total.astype(jnp.bfloat16)

    pieces, partials, arrived = [], [], []
    first, count = 0, 0
    for fetch, width, reduce, lag in PLAN.split():
        first, count = first + count, int(width)
        source = wavefunction
        if int(lag) and len(arrived) >= int(lag):
            source, _ = lax.optimization_barrier((source, arrived[-int(lag)]))
        elif len(partials) >= 2:
            source, _ = lax.optimization_barrier((source, partials[-2]))
        if fetch == "A" and can_share:
            to_upper = picked(source, first, count, is_last)
            to_lower = picked(source, first, count, is_first)
            fetched = lax.ppermute(
                jnp.where(odd == 0, to_upper, to_lower), ("mpo", "sec"), both
            )
            arrived.append(fetched)
            own_side = jnp.where(odd == 0, to_lower, to_upper)
            moved = (
                fetched,
                lax.ppermute(jnp.where(forwards, fetched, own_side), ("mpo", "sec"), passed),
            )
            flags = shared_flags
        else:
            from_lower = lax.ppermute(picked(source, first, count, is_last), "sec", upward)
            from_upper = lax.ppermute(picked(source, first, count, is_first), "sec", downward)
            moved = (from_lower, from_upper)
            arrived.append(moved)
            flags = direct_flags
        partial = apply_rows(
            flags, block_dims, wavefunction, moved, left_env, right_env, first, planes
        )
        partials.append(partial)
        if reduce == "r":
            pieces.append(lax.psum_scatter(partial, "mpo", scatter_dimension=0))
        else:
            pieces.append(sent_sum(partial))
    return jnp.concatenate(pieces, axis=1)


def solution(mesh):
    placed = (
        P(None, "sec", None, None),
        P("mpo", "sec", None, None),
        P("mpo", "sec", None, None),
        P("sec"),
        P("mpo"),
    )
    return jax.shard_map(
        body, mesh=mesh, in_specs=placed, out_specs=P(None, "sec", "mpo", None), check_vma=False
    )
```

```python
import functools

import jax
import jax.numpy as jnp
from jax import lax
from jax.experimental import pallas as pl
from jax.experimental.pallas import tpu as pltpu
from jax.sharding import PartitionSpec as P

COST = 20
PLAN = 'A1s0 D2r1 D2r0 D2r0 D1s0'


def apply_kernel(flags, dims, *refs, first_slot, slots):
    sources, (left, right, out) = refs[:-3], refs[-3:]
    step = pl.program_id(0)
    slot = first_slot + step
    rows = left.shape[0]
    vectors, size = sources[0].shape[0], sources[0].shape[2]
    chunks, slab = out.shape[0], out.shape[3]
    limit = dims[slot]
    row_index = lax.broadcasted_iota(jnp.int32, (size, size), 0)
    col_index = lax.broadcasted_iota(jnp.int32, (size, size), 1)
    inside = jnp.logical_and(row_index < limit, col_index < limit)
    for k in range(vectors):
        parts = []
        for row in range(rows):
            pick, edge = flags[row], flags[rows + row]
            live = jnp.logical_not(
                jnp.logical_or(
                    jnp.logical_and(edge > 0, slot == 0),
                    jnp.logical_and(edge < 0, slot == slots - 1),
                )
            )
            chosen = sources[0][k, 0]
            for i in range(1, len(sources)):
                chosen = jnp.where(pick == i, sources[i][k, 0], chosen)
            chosen = jnp.where(live, chosen, jnp.zeros_like(chosen))
            part = jnp.dot(left[row, 0], chosen, preferred_element_type=jnp.float32)
            parts.append(part.astype(jnp.bfloat16))
        total = jnp.dot(
            jnp.concatenate(parts, axis=1),
            right[:, 0].reshape(rows * size, size),
            preferred_element_type=jnp.float32,
        )
        kept = jnp.where(inside, total, jnp.zeros_like(total)).astype(out.dtype)
        for chunk in range(chunks):
            out[chunk, k, 0] = kept[chunk * slab : (chunk + 1) * slab]


def apply_rows(flags, dims, own, moved, left, right, first_slot, chunks):
    vectors, group, size, _ = moved[0].shape
    rows, slots = left.shape[0], left.shape[1]
    own_spec = pl.BlockSpec((vectors, 1, size, size), lambda i, *_: (0, first_slot + i, 0, 0))
    moved_spec = pl.BlockSpec((vectors, 1, size, size), lambda i, *_: (0, i, 0, 0))
    env_spec = pl.BlockSpec((rows, 1, size, size), lambda i, *_: (0, first_slot + i, 0, 0))
    return pl.pallas_call(
        functools.partial(apply_kernel, first_slot=first_slot, slots=slots),
        grid_spec=pltpu.PrefetchScalarGridSpec(
            num_scalar_prefetch=2,
            grid=(group,),
            in_specs=[own_spec] + [moved_spec] * len(moved) + [env_spec, env_spec],
            out_specs=pl.BlockSpec(
                (chunks, vectors, 1, size // chunks, size), lambda i, *_: (0, 0, i, 0, 0)
            ),
        ),
        out_shape=jax.ShapeDtypeStruct(
            (chunks, vectors, group, size // chunks, size), jnp.bfloat16
        ),
        compiler_params=pltpu.CompilerParams(vmem_limit_bytes=40 * 1024 * 1024),
        cost_estimate=pl.CostEstimate(
            flops=COST * group * vectors * rows * 4 * size**3,
            bytes_accessed=COST * group * size * size * 2 * (4 * vectors + 2 * rows),
            transcendentals=0,
        ),
    )(flags, dims, own, *moved, left, right)


def body(wavefunction, left_env, right_env, block_dims, mpo_shift):
    sec_count, planes = lax.axis_size("sec"), lax.axis_size("mpo")
    sec_index, plane = lax.axis_index("sec"), lax.axis_index("mpo")
    slots = wavefunction.shape[1]
    is_first = (sec_index == 0).astype(jnp.int32)
    is_last = (sec_index == sec_count - 1).astype(jnp.int32)
    odd = plane % 2
    forwards = sec_index % 2 == odd

    edge = jnp.where(mpo_shift > 0, is_first, jnp.where(mpo_shift < 0, -is_last, 0))
    direct_pick = jnp.where(mpo_shift > 0, 1, jnp.where(mpo_shift < 0, 2, 0))
    shared_pick = jnp.where(
        mpo_shift == 0, 0, jnp.where((mpo_shift > 0) == (odd == 0), 1, 2)
    )
    direct_flags = jnp.concatenate([direct_pick, edge]).astype(jnp.int32)
    shared_flags = jnp.concatenate([shared_pick, edge]).astype(jnp.int32)

    upward = [(i, (i + 1) % sec_count) for i in range(sec_count)]
    downward = [(i, (i - 1) % sec_count) for i in range(sec_count)]
    both = [
        (m * sec_count + i, m * sec_count + j)
        for m in range(planes)
        for i, j in (upward if m % 2 == 0 else downward)
    ]
    passed = [
        (m * sec_count + i, (m ^ 1) * sec_count + i if i % 2 == m % 2 else m * sec_count + (i ^ 1))
        for m in range(planes)
        for i in range(sec_count)
    ]
    can_share = planes % 2 == 0 and sec_count % 2 == 0

    def picked(source, first, count, offset):
        step = -1 if offset is is_last else 1
        parts = [
            lax.slice_in_dim(source, at, at + 1, axis=1)
            for at in (min(max(slot + step, 0), slots - 1) for slot in range(first, first + count))
        ]
        plain = lax.slice_in_dim(source, first, first + count, axis=1)
        if 0 <= first + step and first + step + count <= slots:
            moved = lax.slice_in_dim(source, first + step, first + step + count, axis=1)
        else:
            moved = jnp.concatenate(parts, axis=1)
        return jnp.where(offset > 0, moved, plain)

    def sent_sum(partial):
        total = lax.dynamic_index_in_dim(partial, plane, 0, keepdims=False).astype(jnp.float32)
        for distance in range(1, planes):
            target = (plane + distance) % planes
            came = lax.ppermute(
                lax.dynamic_index_in_dim(partial, target, 0, keepdims=False),
                "mpo",
                [(m, (m + distance) % planes) for m in range(planes)],
            )
            total += came.astype(jnp.float32)
        return total.astype(jnp.bfloat16)

    pieces, partials, arrived = [], [], []
    first, count = 0, 0
    for fetch, width, reduce, lag in PLAN.split():
        first, count = first + count, int(width)
        source = wavefunction
        if int(lag) and len(arrived) >= int(lag):
            source, _ = lax.optimization_barrier((source, arrived[-int(lag)]))
        elif len(partials) >= 2:
            source, _ = lax.optimization_barrier((source, partials[-2]))
        if fetch == "A" and can_share:
            to_upper = picked(source, first, count, is_last)
            to_lower = picked(source, first, count, is_first)
            fetched = lax.ppermute(
                jnp.where(odd == 0, to_upper, to_lower), ("mpo", "sec"), both
            )
            arrived.append(fetched)
            own_side = jnp.where(odd == 0, to_lower, to_upper)
            moved = (
                fetched,
                lax.ppermute(jnp.where(forwards, fetched, own_side), ("mpo", "sec"), passed),
            )
            flags = shared_flags
        else:
            from_lower = lax.ppermute(picked(source, first, count, is_last), "sec", upward)
            from_upper = lax.ppermute(picked(source, first, count, is_first), "sec", downward)
            moved = (from_lower, from_upper)
            arrived.append(moved)
            flags = direct_flags
        partial = apply_rows(
            flags, block_dims, wavefunction, moved, left_env, right_env, first, planes
        )
        partials.append(partial)
        if reduce == "r":
            pieces.append(lax.psum_scatter(partial, "mpo", scatter_dimension=0))
        else:
            pieces.append(sent_sum(partial))
    return jnp.concatenate(pieces, axis=1)


def solution(mesh):
    placed = (
        P(None, "sec", None, None),
        P("mpo", "sec", None, None),
        P("mpo", "sec", None, None),
        P("sec"),
        P("mpo"),
    )
    return jax.shard_map(
        body, mesh=mesh, in_specs=placed, out_specs=P(None, "sec", "mpo", None), check_vma=False
    )
```
